512 devices in a mesh: dp: 64 (over z, x), tensor: 8 (over y, core).
Axes of the slice: x: 4, y: 4, z: 16, core: 2. Of those that a mesh axis runs over, the one named last changes fastest.
Arguments:
- grad_out: bfloat16 [32768, 4096], P(('dp', 'tensor')), as said below
- attn_out: bfloat16 [32768, 2048], P('dp', 'tensor'), as said below
Outputs:
- combined: bfloat16 [4096, 2048], P('dp', 'tensor')
Inputs may be any that keep to these rules, and one draw needn't show every extreme that they name: `grad_out`: finite real values. `attn_out`: finite real values.
All inputs are finite; a program needn't handle non-finite values.
Results may differ from the reference program's by a relative error of at most 0.006.
Values may be sent and summed in bfloat16 or wider, within the bound.
A program may use at most 64 MiB of HBM per device.

```python
import math
import jax
import jax.numpy as jnp
from jax import lax

D = 4096
HD = 128
HEADS = 16
TOKR = 512
TOKENS = 32768
N_DP = 64


def draw_grad_out(key, part):
    key = jax.random.fold_in(key, 11)
    key_shared, key_noise, key_scale, key_share, key_weight, key_frac = jax.random.split(key, 6)
    block_share = jax.random.uniform(key_share, (N_DP,), jnp.float32, 0.0, 3.0)
    noise = jax.random.normal(key_noise, (N_DP, TOKR, D), jnp.float32)
    replica_weight = 0.1 * jnp.exp(jax.random.uniform(key_weight, (N_DP,), jnp.float32) * math.log(30.0))
    replica_frac = 0.2 * jnp.exp(jax.random.uniform(key_frac, (N_DP,), jnp.float32) * math.log(10.0))
    col_share = jnp.repeat(block_share, D // N_DP)
    share_table = replica_frac[:, None] * col_share[None, :]
    shared = jax.random.normal(key_shared, (TOKR, D), jnp.float32)
    col_scale = 0.3 * jnp.exp(jax.random.uniform(key_scale, (D,), jnp.float32) * math.log(10.0))
    whole = share_table[:, None, :] * shared[None, :, :] + noise
    norming = replica_weight[:, None] * col_scale[None, :] / jnp.sqrt(TOKR * (1.0 + share_table * share_table))
    return (whole * norming[:, None, :]).reshape(TOKENS, D).astype(jnp.bfloat16)


def draw_attn_out(key, part):
    key = jax.random.fold_in(key, 23)
    key_shared, key_noise, key_scale, key_share = jax.random.split(key, 4)
    head_share = jax.random.uniform(key_share, (HEADS,), jnp.float32, 0.3, 3.0)
    noise = jax.random.normal(key_noise, (TOKENS, HEADS * HD), jnp.float32)
    col_share = jnp.repeat(head_share, HD)
    shared = jax.random.normal(key_shared, (TOKR, HEADS * HD), jnp.float32)
    col_scale = 0.5 * jnp.exp(jax.random.uniform(key_scale, (HEADS * HD,), jnp.float32) * math.log(4.0))
    whole = col_share[None, :] * jnp.tile(shared, (N_DP, 1)) + noise
    norming = col_scale / jnp.sqrt(1.0 + col_share * col_share)
    return (whole * norming[None, :]).astype(jnp.bfloat16)


def setup_inputs(seed: int = 0) -> dict:
    key_of = jax.random.split(jax.random.key(seed), 3)
    return {
        "grad_out": draw_grad_out(jax.random.fold_in(key_of[2], 71), 0),
        "attn_out": draw_attn_out(jax.random.fold_in(key_of[2], 71), 0),
    }


def one_grad(inputs_pair):
    out_rows, attn_rows = inputs_pair
    return jnp.dot(out_rows.T, attn_rows, preferred_element_type=jnp.float32).astype(jnp.bfloat16)

def combine(paired):
    first_f = paired[0].astype(jnp.float32)
    second_f = paired[1].astype(jnp.float32)
    inner_prod = jnp.sum(first_f * second_f)
    first_sq = jnp.sum(first_f * first_f)
    second_sq = jnp.sum(second_f * second_f)
    first_coef = 1.0 - inner_prod / (2.0 * (first_sq + 1e-06))
    second_coef = 1.0 - inner_prod / (2.0 * (second_sq + 1e-06))
    return (first_coef * first_f + second_coef * second_f).astype(jnp.bfloat16)

def reference(grad_out, attn_out):
    out_split = grad_out.reshape(N_DP, TOKR, D)
    attn_split = attn_out.reshape(N_DP, TOKR, HEADS * HD)
    replica_grads = lax.map(one_grad, (out_split, attn_split))
    block_count = N_DP
    while block_count > 1:
        paired_grads = replica_grads.reshape(block_count // 2, 2, D, HEADS * HD)
        replica_grads = lax.map(combine, paired_grads)
        block_count = block_count // 2
    return replica_grads[0]
```

```python
import functools

import jax
import jax.numpy as jnp
from jax import lax
from jax.experimental import pallas as pl
from jax.experimental.pallas import tpu as pltpu
from jax.sharding import PartitionSpec as P

MESH = pl.DeviceIdType.MESH
F32 = jnp.float32
BF16 = jnp.bfloat16

NX, NY, NZ = 4, 4, 16
NT = 2 * NY
EPS = 1e-6
ORDER = (0, 1, 3, 2)


def sum_rows(value):
    rows, lanes = value.shape
    part = value.reshape(rows // 8, 8, lanes).sum(axis=0)
    return sum(part[:, i : i + 128] for i in range(0, lanes, 128))


def coef(inner, own_sq):
    return 1.0 - inner / (2.0 * (jnp.maximum(own_sq, 0.0) + EPS))


def four_weights(p):
    c = [coef(p[i][i ^ 1], p[i][i]) for i in range(4)]

    def paired(i, j):
        return c[i] * (c[j] * p[i][j] + c[j + 1] * p[i][j + 1]) + c[i + 1] * (
            c[j] * p[i + 1][j] + c[j + 1] * p[i + 1][j + 1]
        )

    inner = paired(0, 2)
    low, high = coef(inner, paired(0, 0)), coef(inner, paired(2, 2))
    return [low * c[0], low * c[1], high * c[2], high * c[3]]


def tree_weights(gram):
    row = lax.broadcasted_iota(jnp.int32, gram.shape, 0)
    lane = lax.broadcasted_iota(jnp.int32, gram.shape, 1)
    col = lane & (NZ - 1)
    first = lane < NZ
    weight = None
    step = 1
    while step < NZ:
        diag, pair = col == row, col == (row ^ step)
        c_row = coef(
            jnp.sum(jnp.where(pair & first, gram, 0.0), axis=1, keepdims=True),
            jnp.sum(jnp.where(diag & first, gram, 0.0), axis=1, keepdims=True),
        )
        weight = c_row if weight is None else weight * c_row
        if 2 * step < NZ:
            c_col = coef(
                jnp.sum(jnp.where(pair, gram, 0.0), axis=0, keepdims=True),
                jnp.sum(jnp.where(diag, gram, 0.0), axis=0, keepdims=True),
            )
            gram = c_row * gram * c_col
            gram = gram + jnp.where(
                (row & step) != 0, pltpu.roll(gram, step, 0), pltpu.roll(gram, NZ - step, 0)
            )
            gram = gram + jnp.where(
                (col & step) != 0, pltpu.roll(gram, step, 1), pltpu.roll(gram, 128 - step, 1)
            )
        step *= 2
    return weight


def kernel(
    g_ref, a_ref, o_ref,
    gv, st, gb, ab, lbuf, cb, rb, yb, wv,
    gp1, g1t, g1x, g2t, g2x, g2z,
    in_sem, gs, gr, as_, ar, zs, zr,
    s1t, r1t, s1x, r1x, s2t, r2t, s2x, r2x, s2z, r2z,
):
    dp, t = lax.axis_index("dp"), lax.axis_index("tensor")
    z, x = dp // NX, dp % NX
    y, c = t // 2, t % 2
    tok = g_ref.shape[0]
    half = tok // 2
    block = o_ref.shape[0]

    def x_dev(i):
        return (z * NX + i, t)

    def t_dev(i):
        return (dp, i)

    def z_dev(i):
        return (i * NX + x, t)

    def send(src, dst, ssem, rsem, dev):
        copy = pltpu.make_async_remote_copy(
            src_ref=src, dst_ref=dst, send_sem=ssem, recv_sem=rsem,
            device_id=dev, device_id_type=MESH,
        )
        copy.start()
        return copy

    def arrived(dst, rsem):
        pltpu.make_async_copy(dst, dst, rsem).wait()

    load_g = pltpu.make_async_copy(g_ref, gv, in_sem.at[0])
    load_g.start()
    load_a = pltpu.make_async_copy(a_ref, ab.at[0], in_sem.at[1])
    load_a.start()

    barrier = pltpu.get_barrier_semaphore()
    for k in range(1, NX):
        pl.semaphore_signal(barrier, inc=1, device_id=x_dev((x + k) % NX), device_id_type=MESH)
    for k in range(1, NT):
        pl.semaphore_signal(barrier, inc=1, device_id=t_dev((t + k) % NT), device_id_type=MESH)

    def greet(k, _):
        pl.semaphore_signal(barrier, inc=1, device_id=z_dev((z + k) % NZ), device_id_type=MESH)
        return 0

    lax.fori_loop(1, NZ, greet, 0)

    load_g.wait()
    for i in range(NX):
        for k in range(NZ // 2):
            low, high = 64 * (2 * k * NX + i), 64 * ((2 * k + 1) * NX + i)
            st[i, :, 128 * k : 128 * k + 128] = jnp.concatenate(
                [gv[:, low : low + 64], gv[:, high : high + 64]], axis=1
            )
    mine = pl.ds(t * tok, tok)
    gb[0, mine, :] = st[x]
    load_a.wait()
    pl.semaphore_wait(barrier, NX + NT + NZ - 3)

    sent = []

    def rows(yy, cc, start=0, size=None):
        return pl.ds((yy * 2 + cc) * tok + start, tok if size is None else size)

    up, down, over = (y + 1) % NY, (y + NY - 1) % NY, (y + 2) % NY
    y_up, y_down, core = t_dev(up * 2 + c), t_dev(down * 2 + c), t_dev(y * 2 + 1 - c)

    def spread(d, region, k, dev):
        ref = gb.at[d, region]
        sent.append(send(ref, ref, gs.at[d, k], gr.at[d, k], dev))

    def landed(d, region, k):
        arrived(gb.at[d, region], gr.at[d, k])

    def start_block(d):
        if d:
            landed(d, mine, 0)
        spread(d, mine, 1, y_up)
        spread(d, mine, 2, y_down)
        spread(d, mine, 5, core)

    def forward_near(d):
        landed(d, rows(down, c), 1)
        spread(d, rows(down, c, 0, half), 3, y_up)
        landed(d, rows(up, c), 2)
        spread(d, rows(up, c, half, half), 4, y_down)
        spread(d, rows(down, c), 6, core)
        spread(d, rows(up, c), 7, core)

    def forward_far(d):
        landed(d, rows(over, c, 0, half), 3)
        spread(d, rows(over, c, 0, half), 8, core)
        landed(d, rows(over, c, half, half), 4)
        spread(d, rows(over, c, half, half), 9, core)

    def finish_block(d):
        landed(d, rows(y, 1 - c), 5)
        landed(d, rows(down, 1 - c), 6)
        landed(d, rows(up, 1 - c), 7)
        landed(d, rows(over, 1 - c, 0, half), 8)
        landed(d, rows(over, 1 - c, half, half), 9)

    tile = 256
    lanes = o_ref.shape[1]
    wide = gb.shape[2]

    def compute(d, before):
        r = (x + d) % NX
        others = before + [d]

        def body(i, accs):
            cols = pl.ds(pl.multiple_of(i * tile, tile), tile)
            value = lax.dot_general(
                gb[d, :, cols], ab[d], (((0,), (0,)), ((), ())), preferred_element_type=F32
            )
            lbuf[r, cols, :] = value
            out = []
            for acc, e in zip(accs, others):
                other = value if e == d else lbuf[(x + e) % NX, cols, :]
                out.append(acc + sum_rows(value * other))
            return tuple(out)

        zero = jnp.zeros((8, 128), F32)
        accs = lax.fori_loop(0, wide // tile, body, (zero,) * len(others))
        for acc, e in zip(accs, others):
            q = (x + e) % NX
            line = jnp.sum(acc, axis=0, keepdims=True)
            gp1[pl.ds(r * NX + q, 1), :] = line
            if e != d:
                gp1[pl.ds(q * NX + r, 1), :] = line

    for d in (1, 3, 2):
        sent.append(
            send(st.at[(x + d) % NX], gb.at[NX - d, mine], gs.at[d, 0], gr.at[NX - d, 0], x_dev((x + d) % NX))
        )
    start_block(0)
    right, left = x_dev((x + 1) % NX), x_dev((x + 3) % NX)
    sent.append(send(ab.at[0], ab.at[3], as_.at[0], ar.at[0], right))
    sent.append(send(ab.at[0], ab.at[1], as_.at[1], ar.at[1], left))
    start_block(1)
    start_block(3)
    forward_near(0)
    start_block(2)
    forward_near(1)
    forward_far(0)
    finish_block(0)
    compute(0, [])
    forward_near(3)
    forward_far(1)
    arows = ab.shape[1] // 2
    arrived(ab.at[3], ar.at[0])
    near = ab.at[3, pl.ds(0, arows)], ab.at[2, pl.ds(0, arows)]
    sent.append(send(*near, as_.at[2], ar.at[2], right))
    arrived(ab.at[1], ar.at[1])
    near = ab.at[1, pl.ds(arows, arows)], ab.at[2, pl.ds(arows, arows)]
    sent.append(send(*near, as_.at[3], ar.at[3], left))
    finish_block(1)
    compute(1, [0])
    forward_near(2)
    forward_far(3)
    finish_block(3)
    compute(3, [0, 1])
    forward_far(2)
    arrived(ab.at[2, pl.ds(0, arows)], ar.at[2])
    arrived(ab.at[2, pl.ds(arows, arows)], ar.at[3])
    finish_block(2)
    compute(2, [0, 1, 3])

    def total(buf, value, me, count, dev_of, ssem, rsem):
        buf[me] = value

        def out(k, _):
            send(buf.at[me], buf.at[me], ssem.at[k], rsem.at[me], dev_of((me + k) % count))
            return 0

        def back(k, _):
            q = (me + k) % count
            arrived(buf.at[q], rsem.at[q])
            return 0

        def done(k, _):
            pltpu.make_async_copy(buf.at[me], buf.at[me], ssem.at[k]).wait()
            return 0

        lax.fori_loop(1, count, out, 0)
        lax.fori_loop(1, count, back, 0)
        lax.fori_loop(1, count, done, 0)
        return sum(buf[i] for i in range(count))

    part = total(g1t, gp1[...], t, NT, t_dev, s1t, r1t)
    part = total(g1x, part, x, NX, x_dev, s1x, r1x)
    part = jnp.broadcast_to(jnp.sum(part, axis=1, keepdims=True), part.shape)
    inner = [[part[i * NX + j : i * NX + j + 1] for j in range(NX)] for i in range(NX)]
    w4 = [jnp.concatenate([w] * (lanes // 128), axis=1) for w in four_weights(inner)]

    def combined(b):
        region = pl.ds(pl.multiple_of(b * block, block), block)
        return sum(w4[i] * lbuf[i, region, :] for i in range(NX)).astype(BF16)

    def z_out(k, _):
        b = (z + k) % NZ
        cb[b] = combined(b)
        send(cb.at[b], rb.at[z], zs.at[k], zr.at[z], z_dev(b))
        return 0

    for k in (8, 7, 9, 6, 10, 5, 11, 4, 12, 3, 13, 2, 14, 1, 15):
        z_out(k, 0)
    rb[z] = combined(z)


    for k in (0, 1, 15, 2, 14, 3, 13, 4, 12, 5, 11, 6, 10, 7, 9, 8):
        if k:
            q = (z + k) % NZ
            arrived(rb.at[q], zr.at[q])
        q = (z + k) % NZ
        for i in range(lanes // 128):
            yb[i, pl.ds(q, block, stride=NZ), :] = rb[q, :, 128 * i : 128 * i + 128].astype(F32)

    def square(i, acc):
        for j in range(lanes // 128):
            part = yb[j, pl.ds(pl.multiple_of(i * 128, 128), 128), :].astype(BF16)
            acc = acc + lax.dot_general(
                part, part, (((1,), (1,)), ((), ())), preferred_element_type=F32
            )
        return acc

    gram = lax.fori_loop(0, block * NZ // 128, square, jnp.zeros((128, 128), F32))
    same = (lax.broadcasted_iota(jnp.int32, (128, 128), 0) // NZ) == (
        lax.broadcasted_iota(jnp.int32, (128, 128), 1) // NZ
    )
    gram = jnp.where(same, gram, 0.0).reshape(128 // NZ, NZ, 128).sum(axis=0)
    gram = total(g2t, gram, t, NT, t_dev, s2t, r2t)
    gram = total(g2x, gram, x, NX, x_dev, s2x, r2x)
    gram = total(g2z, gram, z, NZ, z_dev, s2z, r2z)
    for shift in (NZ, 2 * NZ, 4 * NZ):
        gram = gram + pltpu.roll(gram, shift, 1)
    wv[...] = jnp.broadcast_to(tree_weights(gram), (NZ, lanes))
    o_ref[...] = sum(wv[i : i + 1, :] * rb[i].astype(F32) for i in range(NZ)).astype(BF16)

    for copy in sent:
        copy.wait_send()

    def z_done(k, _):
        pltpu.make_async_copy(cb.at[0], cb.at[0], zs.at[k]).wait()
        return 0

    lax.fori_loop(1, NZ, z_done, 0)


def shards(grad_out, attn_out):
    tok, width = grad_out.shape
    rows, lanes = attn_out.shape
    wide, block = width // NX, width // (NX * NZ)
    dma, reg = pltpu.SemaphoreType.DMA, pltpu.VMEM
    return pl.pallas_call(
        kernel,
        out_shape=jax.ShapeDtypeStruct((block, lanes), BF16),
        in_specs=[pl.BlockSpec(memory_space=pl.ANY)] * 2,
        out_specs=pl.BlockSpec(memory_space=pltpu.VMEM),
        scratch_shapes=[
            reg((tok, width), BF16),
            reg((NX, tok, wide), BF16),
            reg((NX, rows, wide), BF16),
            reg((NX, rows, lanes), BF16),
            reg((NX, wide, lanes), F32),
            reg((NZ, block, lanes), BF16),
            reg((NZ, block, lanes), BF16),
            reg((lanes // 128, NZ * block, 128), F32),
            reg((NZ, lanes), F32),
            reg((NX * NX, 128), F32),
            reg((NT, NX * NX, 128), F32),
            reg((NX, NX * NX, 128), F32),
            reg((NT, NZ, 128), F32),
            reg((NX, NZ, 128), F32),
            reg((NZ, NZ, 128), F32),
            dma((2,)),
            dma((NX, 10)), dma((NX, 10)),
            dma((4,)), dma((4,)),
            dma((NZ,)), dma((NZ,)),
            dma((NT,)), dma((NT,)),
            dma((NX,)), dma((NX,)),
            dma((NT,)), dma((NT,)),
            dma((NX,)), dma((NX,)),
            dma((NZ,)), dma((NZ,)),
        ],
        compiler_params=pltpu.CompilerParams(
            collective_id=0, has_side_effects=True, vmem_limit_bytes=40 * 1024 * 1024
        ),
        name="adasum",
    )(grad_out, attn_out)


def solution(mesh):
    return jax.shard_map(
        shards,
        mesh=mesh,
        in_specs=(P(("dp", "tensor"), None), P("dp", "tensor")),
        out_specs=P("dp", "tensor"),
        check_vma=False,
    )
```

```python
import jax
import jax.numpy as jnp
from jax import lax
from jax.experimental import pallas as pl
from jax.experimental.pallas import tpu as pltpu
from jax.sharding import PartitionSpec as P

MESH = pl.DeviceIdType.MESH
F32 = jnp.float32
BF16 = jnp.bfloat16

NX, NY, NZ = 4, 4, 16
NT = 2 * NY
NP = NZ // 2
GROUP = 2 * NX
EPS = 1e-6
ORDER = (0, 1, 3, 4, 2, 5, 7, 6)


def sum_rows(value):
    rows, lanes = value.shape
    part = value.reshape(rows // 8, 8, lanes).sum(axis=0)
    return sum(part[:, i : i + 128] for i in range(0, lanes, 128))


def coef(inner, own_sq):
    return 1.0 - inner / (2.0 * (jnp.maximum(own_sq, 0.0) + EPS))


def pack(lines):
    each = jnp.sum(lines, axis=1, keepdims=True)
    row = lax.broadcasted_iota(jnp.int32, lines.shape, 0)
    lane = lax.broadcasted_iota(jnp.int32, lines.shape, 1)
    return jnp.sum(jnp.where(row == lane, each, 0.0), axis=0, keepdims=True)


def tree_weights(line):
    n = 8
    row = lax.broadcasted_iota(jnp.int32, (n, 128), 0)
    lane = lax.broadcasted_iota(jnp.int32, (n, 128), 1)
    col = lane & (n - 1)
    gram = jnp.where(lane // n == row, jnp.broadcast_to(line, (n, 128)), 0.0)
    for shift in (8, 16, 32, 64):
        gram = gram + pltpu.roll(gram, shift, 1)
    first = lane < n
    weight = None
    step = 1
    while step < n:
        diag, pair = col == row, col == (row ^ step)
        c_row = coef(
            jnp.sum(jnp.where(pair & first, gram, 0.0), axis=1, keepdims=True),
            jnp.sum(jnp.where(diag & first, gram, 0.0), axis=1, keepdims=True),
        )
        weight = c_row if weight is None else weight * c_row
        if 2 * step < n:
            c_col = coef(
                jnp.sum(jnp.where(pair, gram, 0.0), axis=0, keepdims=True),
                jnp.sum(jnp.where(diag, gram, 0.0), axis=0, keepdims=True),
            )
            gram = c_row * gram * c_col
            gram = gram + jnp.where(
                (row & step) != 0, pltpu.roll(gram, step, 0), pltpu.roll(gram, n - step, 0)
            )
            gram = gram + jnp.where(
                (col & step) != 0, pltpu.roll(gram, step, 1), pltpu.roll(gram, 128 - step, 1)
            )
        step *= 2
    return weight


def kernel(
    g_ref, a_ref, o_ref,
    gv, st, gb, ab, lbuf, cb, rb, rf, wv, gp1, gp2,
    line1, slots1, line2, slots2, line3, slots3,
    in_sem, gs, gr, as_, ar, zs, zr, sums,
):
    dp, t = lax.axis_index("dp"), lax.axis_index("tensor")
    z, x = dp // NX, dp % NX
    zp, zb = z // 2, z % 2
    y, c = t // 2, t % 2
    tok = g_ref.shape[0]
    half = tok // 2
    block, lanes = o_ref.shape
    wide = gb.shape[2]

    def dev(xx, zz, tt):
        return (zz * NX + xx, tt)

    def group_dev(i):
        return dev(i // NT % NX, zp * 2 + i // (NT * NX), i % NT)

    def plane_dev(i):
        return dev(i // NT, z, i % NT)

    def z_dev(i):
        return dev(x, i, t)

    me_group, me_plane = (zb * NX + x) * NT + t, x * NT + t

    def send(src, dst, ssem, rsem, to):
        copy = pltpu.make_async_remote_copy(
            src_ref=src, dst_ref=dst, send_sem=ssem, recv_sem=rsem,
            device_id=to, device_id_type=MESH,
        )
        copy.start()
        return copy

    def arrived(dst, rsem):
        pltpu.make_async_copy(dst, dst, rsem).wait()

    load_g = pltpu.make_async_copy(g_ref, gv, in_sem.at[0])
    load_g.start()
    load_a = pltpu.make_async_copy(a_ref, ab.at[0], in_sem.at[1])
    load_a.start()

    barrier = pltpu.get_barrier_semaphore()

    def greet(dev_of, me, count):
        def body(k, _):
            to = dev_of((me + k) % count)
            pl.semaphore_signal(barrier, inc=1, device_id=to, device_id_type=MESH)
            return 0

        lax.fori_loop(1, count, body, 0)

    greet(group_dev, me_group, GROUP * NT)
    greet(z_dev, z, NZ)

    load_g.wait()
    for i in range(NX):
        for k in range(NZ // 2):
            par, pos = k // (NP // 2), 2 * (k % (NP // 2))
            low, high = (64 * (NX * (2 * p + par) + i) for p in (pos, pos + 1))
            st[par * NX + i, :, 64 * pos : 64 * pos + 128] = jnp.concatenate(
                [gv[:, low : low + 64], gv[:, high : high + 64]], axis=1
            )
    mine = pl.ds(t * tok, tok)
    gb[0, mine, :] = st[zb * NX + x]
    load_a.wait()
    pl.semaphore_wait(barrier, GROUP * NT - 1 + NZ - 1)

    sent = []

    def rows(yy, cc, start=0, size=None):
        return pl.ds((yy * 2 + cc) * tok + start, tok if size is None else size)

    def beside(e):
        return (x + e % NX) % NX, zp * 2 + (zb + e // NX) % 2

    up, down, over = (y + 1) % NY, (y + NY - 1) % NY, (y + 2) % NY
    y_up, y_down, core = (dev(x, z, i) for i in (up * 2 + c, down * 2 + c, y * 2 + 1 - c))

    def give(e):
        xx, zz = beside(e)
        back = e // NX * NX + (NX - e % NX) % NX
        src = st.at[zz % 2 * NX + xx]
        sent.append(send(src, gb.at[back, mine], gs.at[e, 0], gr.at[back, 0], dev(xx, zz, t)))

    def spread(e, region, k, to):
        ref = gb.at[e, region]
        sent.append(send(ref, ref, gs.at[e, k], gr.at[e, k], to))

    def landed(e, region, k):
        arrived(gb.at[e, region], gr.at[e, k])

    def start(e):
        if e:
            landed(e, mine, 0)
        spread(e, mine, 1, y_up)
        spread(e, mine, 2, y_down)
        spread(e, mine, 5, core)

    def near(e):
        landed(e, rows(down, c), 1)
        spread(e, rows(down, c, 0, half), 3, y_up)
        landed(e, rows(up, c), 2)
        spread(e, rows(up, c, half, half), 4, y_down)
        spread(e, rows(down, c), 6, core)
        spread(e, rows(up, c), 7, core)

    def far(e):
        landed(e, rows(over, c, 0, half), 3)
        landed(e, rows(over, c, half, half), 4)
        spread(e, rows(over, c), 8, core)

    def whole(e):
        landed(e, rows(y, 1 - c), 5)
        landed(e, rows(down, 1 - c), 6)
        landed(e, rows(up, 1 - c), 7)
        landed(e, rows(over, 1 - c), 8)

    arows = ab.shape[1] // 2
    low, high, full = pl.ds(0, arows), pl.ds(arows, arows), pl.ds(0, 2 * arows)
    right, left = dev((x + 1) % NX, z, t), dev((x + 3) % NX, z, t)
    across = dev(x, zp * 2 + 1 - zb, t)

    def pass_on(e, to_e, part, k, to):
        sent.append(send(ab.at[e, part], ab.at[to_e, part], as_.at[k], ar.at[k], to))

    def have(e, part, k):
        arrived(ab.at[e, part], ar.at[k])

    def heads_start():
        pass_on(0, 3, full, 0, right)
        pass_on(0, 1, full, 1, left)
        pass_on(0, 4, full, 2, across)

    def heads_near():
        have(3, full, 0)
        pass_on(3, 2, low, 3, right)
        pass_on(3, 7, high, 5, across)
        have(1, full, 1)
        pass_on(1, 2, high, 4, left)
        pass_on(1, 5, low, 6, across)

    def heads_across():
        have(4, full, 2)
        pass_on(4, 7, low, 7, right)
        pass_on(4, 5, high, 8, left)

    def heads_far():
        have(7, low, 7)
        pass_on(7, 6, low, 9, right)
        have(5, high, 8)
        pass_on(5, 6, high, 10, left)

    heads_needs = {
        2: ((low, 3), (high, 4)),
        5: ((low, 6),),
        7: ((high, 5),),
        6: ((low, 9), (high, 10)),
    }
    tile = 256

    def index(e):
        return (zb + e // NX) % 2 * NX + (x + e % NX) % NX

    def put(gp, i, j, acc):
        line = jnp.sum(acc, axis=0, keepdims=True)
        gp[pl.ds(i * 8 + j, 1), :] = line
        gp[pl.ds(j * 8 + i, 1), :] = line

    def compute(e, before):
        for part, k in heads_needs.get(e, ()):
            have(e, part, k)
        r = index(e)
        others = before + [e]

        def body(i, accs):
            cols = pl.ds(pl.multiple_of(i * tile, tile), tile)
            value = lax.dot_general(
                gb[e, :, cols], ab[e], (((0,), (0,)), ((), ())), preferred_element_type=F32
            )
            lbuf[r, cols, :] = value
            out = []
            for acc, o in zip(accs, others):
                other = value if o == e else lbuf[index(o), cols, :]
                out.append(acc + sum_rows(value * other))
            return tuple(out)

        zero = jnp.zeros((8, 128), F32)
        accs = lax.fori_loop(0, wide // tile, body, (zero,) * len(others))
        for acc, o in zip(accs, others):
            put(gp1, r, index(o), acc)

    for e in ORDER[1:]:
        give(e)
    start(0)
    done = []

    def finish(e):
        whole(e)
        compute(e, list(done))
        done.append(e)

    start(1)
    start(3)
    start(4)
    heads_start()
    near(0)
    start(2)
    start(5)
    start(7)
    near(1)
    far(0)
    start(6)
    near(3)
    far(1)
    finish(0)
    near(4)
    far(3)
    heads_across()
    heads_near()
    finish(1)
    near(2)
    far(4)
    finish(3)
    near(5)
    far(2)
    finish(4)
    near(7)
    far(5)
    heads_far()
    near(6)
    finish(2)
    far(7)
    finish(5)
    far(6)
    finish(7)
    finish(6)

    def total(line, slots, value, me, count, dev_of, k):
        line[...] = value
        keep = pltpu.make_async_copy(line, slots.at[pl.ds(me, 1)], sums.at[k, 1])
        keep.start()

        def out(i, _):
            send(line, slots.at[pl.ds(me, 1)], sums.at[k, 0], sums.at[k, 1], dev_of((me + i) % count))
            return 0

        lax.fori_loop(1, count, out, 0)
        every = slots.at[pl.ds(0, count)]
        pltpu.make_async_copy(every, every, sums.at[k, 1]).wait()
        others = slots.at[pl.ds(0, count - 1)]
        pltpu.make_async_copy(others, others, sums.at[k, 0]).wait()
        return jnp.sum(slots[...], axis=0, keepdims=True)

    line = total(line1, slots1, pack(gp1[...]), me_group, GROUP * NT, group_dev, 0)
    wv[...] = jnp.broadcast_to(tree_weights(line), wv.shape)
    w8 = [wv[i : i + 1, :] for i in range(GROUP)]

    def combined(b):
        region = pl.ds(pl.multiple_of(b * block, block), block)
        return sum(w8[i] * lbuf[i, region, :] for i in range(GROUP)).astype(BF16)

    for k in (4, 3, 5, 2, 6, 1, 7):
        b = (zp + k) % NP
        cb[b] = combined(b)
        sent.append(send(cb.at[b], rb.at[zp], zs.at[k], zr.at[zp], z_dev(2 * b + zb)))
    rb[zp] = combined(zp)

    places = []
    for k in (0, 1, 7, 2, 6, 3, 5, 4):
        q = (zp + k) % NP
        if k:
            arrived(rb.at[q], zr.at[q])
        value = rb[q].astype(F32)
        rf[q] = value
        for o in places:
            put(gp2, q, o, sum_rows(value * rf[o]))
        put(gp2, q, q, sum_rows(value * value))
        places.append(q)

    line = total(line2, slots2, pack(gp2[...]), me_plane, NX * NT, plane_dev, 1)
    line = total(line3, slots3, line, z, NZ, z_dev, 2)
    wv[...] = jnp.broadcast_to(tree_weights(line), wv.shape)
    o_ref[...] = sum(wv[i : i + 1, :] * rf[i] for i in range(NP)).astype(BF16)

    for copy in sent:
        copy.wait_send()


def shards(grad_out, attn_out):
    tok, width = grad_out.shape
    rows, lanes = attn_out.shape
    wide, block = width // GROUP, width // (NX * NZ)
    dma, reg = pltpu.SemaphoreType.DMA, pltpu.VMEM
    return pl.pallas_call(
        kernel,
        out_shape=jax.ShapeDtypeStruct((block, lanes), BF16),
        in_specs=[pl.BlockSpec(memory_space=pl.ANY)] * 2,
        out_specs=pl.BlockSpec(memory_space=pltpu.VMEM),
        scratch_shapes=[
            reg((tok, width), BF16),
            reg((GROUP, tok, wide), BF16),
            reg((GROUP, rows, wide), BF16),
            reg((GROUP, rows, lanes), BF16),
            reg((GROUP, wide, lanes), F32),
            reg((NP, block, lanes), BF16),
            reg((NP, block, lanes), BF16),
            reg((NP, block, lanes), F32),
            reg((8, lanes), F32),
            reg((64, 128), F32),
            reg((64, 128), F32),
            reg((1, 128), F32), reg((GROUP * NT, 128), F32),
            reg((1, 128), F32), reg((NX * NT, 128), F32),
            reg((1, 128), F32), reg((NZ, 128), F32),
            dma((2,)),
            dma((GROUP, 9)), dma((GROUP, 9)),
            dma((11,)), dma((11,)),
            dma((NP,)), dma((NP,)),
            dma((3, 2)),
        ],
        compiler_params=pltpu.CompilerParams(
            collective_id=0, has_side_effects=True, vmem_limit_bytes=60 * 1024 * 1024
        ),
        name="adasum",
    )(grad_out, attn_out)


def solution(mesh):
    return jax.shard_map(
        shards,
        mesh=mesh,
        in_specs=(P(("dp", "tensor"), None), P("dp", "tensor")),
        out_specs=P("dp", "tensor"),
        check_vma=False,
    )
```

```python
import jax
import jax.numpy as jnp
from jax import lax
from jax.experimental import pallas as pl
from jax.experimental.pallas import tpu as pltpu
from jax.sharding import PartitionSpec as P

MESH = pl.DeviceIdType.MESH
F32 = jnp.float32
BF16 = jnp.bfloat16

NX, NY, NZ = 4, 4, 16
NT = 2 * NY
NP = NZ // 2
GROUP = 2 * NX
EPS = 1e-6
ORDER = (0, 1, 3, 4, 5, 7, 2, 6)
AHEAD = 4
DIRECT = (0, 6)
HEADS = (3, 5)


def sum_rows(value):
    rows, lanes = value.shape
    part = value.reshape(rows // 8, 8, lanes).sum(axis=0)
    return sum(part[:, i : i + 128] for i in range(0, lanes, 128))


def coef(inner, own_sq):
    return 1.0 - inner / (2.0 * (jnp.maximum(own_sq, 0.0) + EPS))


def pack(lines):
    each = jnp.sum(lines, axis=1, keepdims=True)
    row = lax.broadcasted_iota(jnp.int32, lines.shape, 0)
    lane = lax.broadcasted_iota(jnp.int32, lines.shape, 1)
    return jnp.sum(jnp.where(row == lane, each, 0.0), axis=0, keepdims=True)


def tree_weights(line):
    n = 8
    row = lax.broadcasted_iota(jnp.int32, (n, 128), 0)
    lane = lax.broadcasted_iota(jnp.int32, (n, 128), 1)
    col = lane & (n - 1)
    gram = jnp.where(lane // n == row, jnp.broadcast_to(line, (n, 128)), 0.0)
    for shift in (8, 16, 32, 64):
        gram = gram + pltpu.roll(gram, shift, 1)
    first = lane < n
    weight = None
    step = 1
    while step < n:
        diag, pair = col == row, col == (row ^ step)
        c_row = coef(
            jnp.sum(jnp.where(pair & first, gram, 0.0), axis=1, keepdims=True),
            jnp.sum(jnp.where(diag & first, gram, 0.0), axis=1, keepdims=True),
        )
        weight = c_row if weight is None else weight * c_row
        if 2 * step < n:
            c_col = coef(
                jnp.sum(jnp.where(pair, gram, 0.0), axis=0, keepdims=True),
                jnp.sum(jnp.where(diag, gram, 0.0), axis=0, keepdims=True),
            )
            gram = c_row * gram * c_col
            gram = gram + jnp.where(
                (row & step) != 0, pltpu.roll(gram, step, 0), pltpu.roll(gram, n - step, 0)
            )
            gram = gram + jnp.where(
                (col & step) != 0, pltpu.roll(gram, step, 1), pltpu.roll(gram, 128 - step, 1)
            )
        step *= 2
    return weight


def kernel(
    g_ref, a_ref, o_ref,
    gv, st, gb, ab, lbuf, cb, rb, rf, wv, gp1, gp2,
    line1, slots1, line2, slots2, line3, slots3,
    in_sem, gs, gr, as_, ar, zs, zr, sums, heard,
):
    dp, t = lax.axis_index("dp"), lax.axis_index("tensor")
    z, x = dp // NX, dp % NX
    zp, zb = z // 2, z % 2
    y, c = t // 2, t % 2
    tok = g_ref.shape[0]
    half = tok // 2
    block, lanes = o_ref.shape
    wide = gb.shape[2]

    def dev(xx, zz, tt):
        return (zz * NX + xx, tt)

    def group_dev(i):
        return dev(i // NT % NX, zp * 2 + i // (NT * NX), i % NT)

    def plane_dev(i):
        return dev(i // NT, z, i % NT)

    def z_dev(i):
        return dev(x, i, t)

    me_group, me_plane = (zb * NX + x) * NT + t, x * NT + t

    def send(src, dst, ssem, rsem, to):
        copy = pltpu.make_async_remote_copy(
            src_ref=src, dst_ref=dst, send_sem=ssem, recv_sem=rsem,
            device_id=to, device_id_type=MESH,
        )
        copy.start()
        return copy

    def arrived(dst, rsem):
        pltpu.make_async_copy(dst, dst, rsem).wait()

    load_g = pltpu.make_async_copy(g_ref, gv, in_sem.at[0])
    load_g.start()
    load_a = pltpu.make_async_copy(a_ref, ab.at[0], in_sem.at[1])
    load_a.start()

    barrier = pltpu.get_barrier_semaphore()

    up, down, over = (y + 1) % NY, (y + NY - 1) % NY, (y + 2) % NY
    y_up, y_down, core = (dev(x, z, i) for i in (up * 2 + c, down * 2 + c, y * 2 + 1 - c))
    z_up, z_down = z_dev((z + 2) % NZ), z_dev((z + NZ - 2) % NZ)

    def beside(e):
        return (x + e % NX) % NX, zp * 2 + (zb + e // NX) % 2

    def greet(k, _):
        to = group_dev((me_group + k) % (GROUP * NT))
        pl.semaphore_signal(barrier, inc=1, device_id=to, device_id_type=MESH)
        return 0

    lax.fori_loop(1, GROUP * NT, greet, 0)
    for to in (z_up, z_down):
        pl.semaphore_signal(barrier, inc=1, device_id=to, device_id_type=MESH)

    load_g.wait()
    for i in range(NX):
        for k in range(NZ // 2):
            par, pos = k // (NP // 2), 2 * (k % (NP // 2))
            low, high = (64 * (NX * (2 * p + par) + i) for p in (pos, pos + 1))
            st[par * NX + i, :, 64 * pos : 64 * pos + 128] = jnp.concatenate(
                [gv[:, low : low + 64], gv[:, high : high + 64]], axis=1
            )
    mine = pl.ds(t * tok, tok)
    gb[0, mine, :] = st[zb * NX + x]
    load_a.wait()
    pl.semaphore_wait(barrier, GROUP * NT + 1)

    sent = []

    def rows(yy, cc, start=0, size=None):
        return pl.ds((yy * 2 + cc) * tok + start, tok if size is None else size)

    def give(e):
        xx, zz = beside(e)
        back = e // NX * NX + (NX - e % NX) % NX
        src = st.at[zz % 2 * NX + xx]
        sent.append(send(src, gb.at[back, mine], gs.at[e, 0], gr.at[back, 0], dev(xx, zz, t)))

    def spread(e, region, k, to):
        ref = gb.at[e, region]
        sent.append(send(ref, ref, gs.at[e, k], gr.at[e, k], to))

    def landed(e, region, k):
        arrived(gb.at[e, region], gr.at[e, k])

    def start(e):
        if e:
            landed(e, mine, 0)
        spread(e, mine, 1, y_up)
        spread(e, mine, 2, y_down)
        if e in DIRECT:
            spread(e, mine, 3, dev(x, z, over * 2 + c))
        spread(e, mine, 5, core)

    def near(e):
        landed(e, rows(down, c), 1)
        if e not in DIRECT:
            spread(e, rows(down, c, 0, half), 3, y_up)
        landed(e, rows(up, c), 2)
        if e not in DIRECT:
            spread(e, rows(up, c, half, half), 4, y_down)
        spread(e, rows(down, c), 6, core)
        spread(e, rows(up, c), 7, core)

    def far(e):
        if e in DIRECT:
            landed(e, rows(over, c), 3)
        else:
            landed(e, rows(over, c, 0, half), 3)
            landed(e, rows(over, c, half, half), 4)
        spread(e, rows(over, c), 8, core)

    def whole(e):
        landed(e, rows(y, 1 - c), 5)
        landed(e, rows(down, 1 - c), 6)
        landed(e, rows(up, 1 - c), 7)
        landed(e, rows(over, 1 - c), 8)

    arows = ab.shape[1] // 2
    low, high, full = pl.ds(0, arows), pl.ds(arows, arows), pl.ds(0, 2 * arows)
    right, left = dev((x + 1) % NX, z, t), dev((x + 3) % NX, z, t)
    across = dev(x, zp * 2 + 1 - zb, t)

    def pass_on(e, to_e, part, k, to):
        sent.append(send(ab.at[e, part], ab.at[to_e, part], as_.at[k], ar.at[k], to))

    def have(e, part, k):
        arrived(ab.at[e, part], ar.at[k])

    def heads_start():
        pass_on(0, 3, full, 0, right)
        pass_on(0, 1, full, 1, left)
        pass_on(0, 4, full, 2, across)

    def heads_near():
        have(3, full, 0)
        pass_on(3, 2, low, 3, right)
        pass_on(3, 7, high, 5, across)
        have(1, full, 1)
        pass_on(1, 2, high, 4, left)
        pass_on(1, 5, low, 6, across)

    def heads_across():
        have(4, full, 2)
        pass_on(4, 7, low, 7, right)
        pass_on(4, 5, high, 8, left)

    def heads_far():
        have(7, low, 7)
        pass_on(7, 6, low, 9, right)
        have(5, high, 8)
        pass_on(5, 6, high, 10, left)

    heads_needs = {
        2: ((low, 3), (high, 4)),
        5: ((low, 6),),
        7: ((high, 5),),
        6: ((low, 9), (high, 10)),
    }
    tile = 256

    def index(e):
        return (zb + e // NX) % 2 * NX + (x + e % NX) % NX

    def put(gp, i, j, acc):
        line = jnp.sum(acc, axis=0, keepdims=True)
        gp[pl.ds(i * 8 + j, 1), :] = line
        gp[pl.ds(j * 8 + i, 1), :] = line

    def compute(e, before):
        for part, k in heads_needs.get(e, ()):
            have(e, part, k)
        r = index(e)
        others = before + [e]

        def body(i, accs):
            cols = pl.ds(pl.multiple_of(i * tile, tile), tile)
            value = lax.dot_general(
                gb[e, :, cols], ab[e], (((0,), (0,)), ((), ())), preferred_element_type=F32
            )
            lbuf[r, cols, :] = value
            out = []
            for acc, o in zip(accs, others):
                other = value if o == e else lbuf[index(o), cols, :]
                out.append(acc + sum_rows(value * other))
            return tuple(out)

        zero = jnp.zeros((8, 128), F32)
        accs = lax.fori_loop(0, wide // tile, body, (zero,) * len(others))
        for acc, o in zip(accs, others):
            put(gp1, r, index(o), acc)

    done = []

    def finish(e):
        whole(e)
        compute(e, list(done))
        done.append(e)

    def hear(step):
        if step > 1:
            pl.semaphore_wait(heard.at[step - 2, 0], 1)
            pl.semaphore_wait(heard.at[step - 2, 1], 1)
        if step < NP // 2:
            for side, to in enumerate((z_up, z_down)):
                pl.semaphore_signal(heard.at[step - 1, side], inc=1, device_id=to, device_id_type=MESH)

    for e in ORDER[1:AHEAD]:
        give(e)
    for e in ORDER[:AHEAD]:
        start(e)
    for e in ORDER[AHEAD:]:
        give(e)
    heads_start()
    hear(1)
    for i in range(GROUP):
        near(ORDER[i])
        if i + AHEAD < GROUP:
            start(ORDER[i + AHEAD])
        if i == HEADS[0]:
            heads_across()
            heads_near()
        if i == HEADS[1]:
            heads_far()
        if i >= 2:
            far(ORDER[i - 2])
        if i >= 3:
            finish(ORDER[i - 3])
        if 3 <= i < 6:
            hear(i - 1)
    far(ORDER[6])
    finish(ORDER[5])
    far(ORDER[7])
    finish(ORDER[6])
    finish(ORDER[7])

    def total(line, slots, value, me, count, dev_of, k):
        line[...] = value
        keep = pltpu.make_async_copy(line, slots.at[pl.ds(me, 1)], sums.at[k, 1])
        keep.start()

        def out(i, _):
            send(line, slots.at[pl.ds(me, 1)], sums.at[k, 0], sums.at[k, 1], dev_of((me + i) % count))
            return 0

        lax.fori_loop(1, count, out, 0)
        every = slots.at[pl.ds(0, count)]
        pltpu.make_async_copy(every, every, sums.at[k, 1]).wait()
        others = slots.at[pl.ds(0, count - 1)]
        pltpu.make_async_copy(others, others, sums.at[k, 0]).wait()
        return jnp.sum(slots[...], axis=0, keepdims=True)

    line = total(line1, slots1, pack(gp1[...]), me_group, GROUP * NT, group_dev, 0)
    wv[...] = jnp.broadcast_to(tree_weights(line), wv.shape)
    w8 = [wv[i : i + 1, :] for i in range(GROUP)]

    def combined(b):
        region = pl.ds(pl.multiple_of(b * block, block), block)
        return sum(w8[i] * lbuf[i, region, :] for i in range(GROUP)).astype(BF16)

    for k in (4, 3, 5, 2, 6, 1, 7):
        b = (zp + k) % NP
        cb[b] = combined(b)
        sent.append(send(cb.at[b], rb.at[zp], zs.at[k], zr.at[zp], z_dev(2 * b + zb)))
    rb[zp] = combined(zp)

    places = []
    for k in (0, 1, 7, 2, 6, 3, 5, 4):
        q = (zp + k) % NP
        if k:
            arrived(rb.at[q], zr.at[q])
        value = rb[q].astype(F32)
        rf[q] = value
        for o in places:
            put(gp2, q, o, sum_rows(value * rf[o]))
        put(gp2, q, q, sum_rows(value * value))
        places.append(q)

    line = total(line2, slots2, pack(gp2[...]), me_plane, NX * NT, plane_dev, 1)
    line = total(line3, slots3, line, z, NZ, z_dev, 2)
    wv[...] = jnp.broadcast_to(tree_weights(line), wv.shape)
    o_ref[...] = sum(wv[i : i + 1, :] * rf[i] for i in range(NP)).astype(BF16)

    for copy in sent:
        copy.wait_send()


def shards(grad_out, attn_out):
    tok, width = grad_out.shape
    rows, lanes = attn_out.shape
    wide, block = width // GROUP, width // (NX * NZ)
    dma, reg = pltpu.SemaphoreType.DMA, pltpu.VMEM
    return pl.pallas_call(
        kernel,
        out_shape=jax.ShapeDtypeStruct((block, lanes), BF16),
        in_specs=[pl.BlockSpec(memory_space=pl.ANY)] * 2,
        out_specs=pl.BlockSpec(memory_space=pltpu.VMEM),
        scratch_shapes=[
            reg((tok, width), BF16),
            reg((GROUP, tok, wide), BF16),
            reg((GROUP, rows, wide), BF16),
            reg((GROUP, rows, lanes), BF16),
            reg((GROUP, wide, lanes), F32),
            reg((NP, block, lanes), BF16),
            reg((NP, block, lanes), BF16),
            reg((NP, block, lanes), F32),
            reg((8, lanes), F32),
            reg((64, 128), F32),
            reg((64, 128), F32),
            reg((1, 128), F32), reg((GROUP * NT, 128), F32),
            reg((1, 128), F32), reg((NX * NT, 128), F32),
            reg((1, 128), F32), reg((NZ, 128), F32),
            dma((2,)),
            dma((GROUP, 9)), dma((GROUP, 9)),
            dma((11,)), dma((11,)),
            dma((NP,)), dma((NP,)),
            dma((3, 2)),
            pltpu.SemaphoreType.REGULAR((NP // 2 - 1, 2)),
        ],
        compiler_params=pltpu.CompilerParams(
            collective_id=0, has_side_effects=True, vmem_limit_bytes=60 * 1024 * 1024
        ),
        name="adasum",
    )(grad_out, attn_out)


def solution(mesh):
    return jax.shard_map(
        shards,
        mesh=mesh,
        in_specs=(P(("dp", "tensor"), None), P("dp", "tensor")),
        out_specs=P("dp", "tensor"),
        check_vma=False,
    )
```

```python
import jax
import jax.numpy as jnp
from jax import lax
from jax.experimental import pallas as pl
from jax.experimental.pallas import tpu as pltpu
from jax.sharding import PartitionSpec as P

MESH = pl.DeviceIdType.MESH
F32 = jnp.float32
BF16 = jnp.bfloat16

NX, NY, NZ = 4, 4, 16
NT = 2 * NY
NP = NZ // 2
GROUP = 2 * NX
EPS = 1e-6
VMEM = 55040 * 1024
ORDER = (0, 1, 3, 4, 5, 7, 2, 6)
AHEAD = 4
DIRECT = (0, 6)
HEADS = (3, 5)


def sum_rows(value):
    rows, lanes = value.shape
    part = value.reshape(rows // 8, 8, lanes).sum(axis=0)
    return sum(part[:, i : i + 128] for i in range(0, lanes, 128))


def coef(inner, own_sq):
    return 1.0 - inner / (2.0 * (jnp.maximum(own_sq, 0.0) + EPS))


def pack(lines):
    each = jnp.sum(lines, axis=1, keepdims=True)
    row = lax.broadcasted_iota(jnp.int32, lines.shape, 0)
    lane = lax.broadcasted_iota(jnp.int32, lines.shape, 1)
    return jnp.sum(jnp.where(row == lane, each, 0.0), axis=0, keepdims=True)


def tree_weights(line):
    n = 8
    row = lax.broadcasted_iota(jnp.int32, (n, 128), 0)
    lane = lax.broadcasted_iota(jnp.int32, (n, 128), 1)
    col = lane & (n - 1)
    gram = jnp.where(lane // n == row, jnp.broadcast_to(line, (n, 128)), 0.0)
    for shift in (8, 16, 32, 64):
        gram = gram + pltpu.roll(gram, shift, 1)
    first = lane < n
    weight = None
    step = 1
    while step < n:
        diag, pair = col == row, col == (row ^ step)
        c_row = coef(
            jnp.sum(jnp.where(pair & first, gram, 0.0), axis=1, keepdims=True),
            jnp.sum(jnp.where(diag & first, gram, 0.0), axis=1, keepdims=True),
        )
        weight = c_row if weight is None else weight * c_row
        if 2 * step < n:
            c_col = coef(
                jnp.sum(jnp.where(pair, gram, 0.0), axis=0, keepdims=True),
                jnp.sum(jnp.where(diag, gram, 0.0), axis=0, keepdims=True),
            )
            gram = c_row * gram * c_col
            gram = gram + jnp.where(
                (row & step) != 0, pltpu.roll(gram, step, 0), pltpu.roll(gram, n - step, 0)
            )
            gram = gram + jnp.where(
                (col & step) != 0, pltpu.roll(gram, step, 1), pltpu.roll(gram, 128 - step, 1)
            )
        step *= 2
    return weight


def kernel(
    g_ref, a_ref, o_ref,
    gv, st, gb, ab, lbuf, cb, rb, rf, wv, gp1, gp2,
    line1, slots1, line2, slots2, line3, slots3,
    in_sem, gs, gr, as_, ar, zs, zr, sums, heard,
):
    dp, t = lax.axis_index("dp"), lax.axis_index("tensor")
    z, x = dp // NX, dp % NX
    zp, zb = z // 2, z % 2
    y, c = t // 2, t % 2
    tok = g_ref.shape[0]
    half = tok // 2
    block, lanes = o_ref.shape
    wide = gb.shape[2]

    def dev(xx, zz, tt):
        return (zz * NX + xx, tt)

    def group_dev(i):
        return dev(i // NT % NX, zp * 2 + i // (NT * NX), i % NT)

    def plane_dev(i):
        return dev(i // NT, z, i % NT)

    def z_dev(i):
        return dev(x, i, t)

    me_group, me_plane = (zb * NX + x) * NT + t, x * NT + t

    def send(src, dst, ssem, rsem, to):
        copy = pltpu.make_async_remote_copy(
            src_ref=src, dst_ref=dst, send_sem=ssem, recv_sem=rsem,
            device_id=to, device_id_type=MESH,
        )
        copy.start()
        return copy

    def arrived(dst, rsem):
        pltpu.make_async_copy(dst, dst, rsem).wait()

    load_g = pltpu.make_async_copy(g_ref, gv, in_sem.at[0])
    load_g.start()
    load_a = pltpu.make_async_copy(a_ref, ab.at[0], in_sem.at[1])
    load_a.start()

    barrier = pltpu.get_barrier_semaphore()

    up, down, over = (y + 1) % NY, (y + NY - 1) % NY, (y + 2) % NY
    y_up, y_down, y_over = (dev(x, z, i * 2 + c) for i in (up, down, over))
    core = dev(x, z, y * 2 + 1 - c)
    z_up, z_down = z_dev((z + 2) % NZ), z_dev((z + NZ - 2) % NZ)

    def beside(e):
        return (x + e % NX) % NX, zp * 2 + (zb + e // NX) % 2

    greeted = [dev(*beside(e), t) for e in ORDER[1:]] + [y_up, y_down, y_over, core, z_up, z_down]
    for to in greeted:
        pl.semaphore_signal(barrier, inc=1, device_id=to, device_id_type=MESH)

    load_g.wait()
    for i in range(NX):
        for k in range(NZ // 2):
            par, pos = k // (NP // 2), 2 * (k % (NP // 2))
            low, high = (64 * (NX * (2 * p + par) + i) for p in (pos, pos + 1))
            st[par * NX + i, :, 64 * pos : 64 * pos + 128] = jnp.concatenate(
                [gv[:, low : low + 64], gv[:, high : high + 64]], axis=1
            )
    mine = pl.ds(t * tok, tok)
    gb[0, mine, :] = st[zb * NX + x]
    load_a.wait()
    pl.semaphore_wait(barrier, len(greeted))

    sent = []

    def rows(yy, cc, start=0, size=None):
        return pl.ds((yy * 2 + cc) * tok + start, tok if size is None else size)

    def give(e):
        xx, zz = beside(e)
        back = e // NX * NX + (NX - e % NX) % NX
        src = st.at[zz % 2 * NX + xx]
        sent.append(send(src, gb.at[back, mine], gs.at[e, 0], gr.at[back, 0], dev(xx, zz, t)))

    def spread(e, region, k, to):
        ref = gb.at[e, region]
        sent.append(send(ref, ref, gs.at[e, k], gr.at[e, k], to))

    def landed(e, region, k):
        arrived(gb.at[e, region], gr.at[e, k])

    def start(e):
        if e:
            landed(e, mine, 0)
        spread(e, mine, 1, y_up)
        spread(e, mine, 2, y_down)
        if e in DIRECT:
            spread(e, mine, 3, y_over)
        spread(e, mine, 5, core)

    def near(e):
        landed(e, rows(down, c), 1)
        if e not in DIRECT:
            spread(e, rows(down, c, 0, half), 3, y_up)
        landed(e, rows(up, c), 2)
        if e not in DIRECT:
            spread(e, rows(up, c, half, half), 4, y_down)
        spread(e, rows(down, c), 6, core)
        spread(e, rows(up, c), 7, core)

    def far(e):
        if e in DIRECT:
            landed(e, rows(over, c), 3)
        else:
            landed(e, rows(over, c, 0, half), 3)
            landed(e, rows(over, c, half, half), 4)
        spread(e, rows(over, c), 8, core)

    def whole(e):
        landed(e, rows(y, 1 - c), 5)
        landed(e, rows(down, 1 - c), 6)
        landed(e, rows(up, 1 - c), 7)
        landed(e, rows(over, 1 - c), 8)

    arows = ab.shape[1] // 2
    low, high, full = pl.ds(0, arows), pl.ds(arows, arows), pl.ds(0, 2 * arows)
    right, left = dev((x + 1) % NX, z, t), dev((x + 3) % NX, z, t)
    across = dev(x, zp * 2 + 1 - zb, t)

    def pass_on(e, to_e, part, k, to):
        sent.append(send(ab.at[e, part], ab.at[to_e, part], as_.at[k], ar.at[k], to))

    def have(e, part, k):
        arrived(ab.at[e, part], ar.at[k])

    def heads_start():
        pass_on(0, 3, full, 0, right)
        pass_on(0, 1, full, 1, left)
        pass_on(0, 4, full, 2, across)

    def heads_near():
        have(3, full, 0)
        pass_on(3, 2, low, 3, right)
        pass_on(3, 7, high, 5, across)
        have(1, full, 1)
        pass_on(1, 2, high, 4, left)
        pass_on(1, 5, low, 6, across)

    def heads_across():
        have(4, full, 2)
        pass_on(4, 7, low, 7, right)
        pass_on(4, 5, high, 8, left)

    def heads_far():
        have(7, low, 7)
        pass_on(7, 6, low, 9, right)
        have(5, high, 8)
        pass_on(5, 6, high, 10, left)

    heads_needs = {
        2: ((low, 3), (high, 4)),
        5: ((low, 6),),
        7: ((high, 5),),
        6: ((low, 9), (high, 10)),
    }
    tile = 256

    def index(e):
        return (zb + e // NX) % 2 * NX + (x + e % NX) % NX

    def put(gp, i, j, acc):
        line = jnp.sum(acc, axis=0, keepdims=True)
        gp[pl.ds(i * 8 + j, 1), :] = line
        gp[pl.ds(j * 8 + i, 1), :] = line

    def compute(e, before):
        for part, k in heads_needs.get(e, ()):
            have(e, part, k)
        r = index(e)
        others = before + [e]

        def body(i, accs):
            cols = pl.ds(pl.multiple_of(i * tile, tile), tile)
            value = lax.dot_general(
                gb[e, :, cols], ab[e], (((0,), (0,)), ((), ())), preferred_element_type=F32
            )
            lbuf[r, cols, :] = value
            out = []
            for acc, o in zip(accs, others):
                other = value if o == e else lbuf[index(o), cols, :]
                out.append(acc + sum_rows(value * other))
            return tuple(out)

        zero = jnp.zeros((8, 128), F32)
        accs = lax.fori_loop(0, wide // tile, body, (zero,) * len(others))
        for acc, o in zip(accs, others):
            put(gp1, r, index(o), acc)

    done = []

    def finish(e):
        whole(e)
        compute(e, list(done))
        done.append(e)

    def hear(step):
        if step > 1:
            for side in range(5):
                pl.semaphore_wait(heard.at[step - 2, side], 1)
        if step < NP // 2:
            for side, to in enumerate((z_up, z_down, y_up, y_down, core)):
                pl.semaphore_signal(heard.at[step - 1, side], inc=1, device_id=to, device_id_type=MESH)

    for e in ORDER[1:AHEAD]:
        give(e)
    start(0)
    for copy in sent[:AHEAD - 1]:
        copy.wait_send()
    del sent[:AHEAD - 1]
    for e in ORDER[AHEAD:]:
        give(e)
    heads_start()
    for e in ORDER[1:AHEAD]:
        start(e)
    hear(1)
    for i in range(GROUP):
        near(ORDER[i])
        if i + AHEAD < GROUP:
            start(ORDER[i + AHEAD])
        if i == HEADS[0]:
            heads_across()
            heads_near()
        if i == HEADS[1]:
            heads_far()
        if i >= 2:
            far(ORDER[i - 2])
        if i >= 3:
            finish(ORDER[i - 3])
        if 3 <= i < 6:
            hear(i - 1)
    far(ORDER[6])
    finish(ORDER[5])
    far(ORDER[7])
    finish(ORDER[6])
    finish(ORDER[7])

    def total(line, slots, value, me, count, dev_of, k):
        line[...] = value
        keep = pltpu.make_async_copy(line, slots.at[pl.ds(me, 1)], sums.at[k, 1])
        keep.start()

        def out(i, _):
            send(line, slots.at[pl.ds(me, 1)], sums.at[k, 0], sums.at[k, 1], dev_of((me + i) % count))
            return 0

        lax.fori_loop(1, count, out, 0)
        every = slots.at[pl.ds(0, count)]
        pltpu.make_async_copy(every, every, sums.at[k, 1]).wait()
        others = slots.at[pl.ds(0, count - 1)]
        pltpu.make_async_copy(others, others, sums.at[k, 0]).wait()
        return jnp.sum(slots[...], axis=0, keepdims=True)

    line = total(line1, slots1, pack(gp1[...]), me_group, GROUP * NT, group_dev, 0)
    wv[...] = jnp.broadcast_to(tree_weights(line), wv.shape)
    w8 = [wv[i : i + 1, :] for i in range(GROUP)]

    def combined(b):
        region = pl.ds(pl.multiple_of(b * block, block), block)
        return sum(w8[i] * lbuf[i, region, :] for i in range(GROUP)).astype(BF16)

    for k in (4, 3, 5, 2, 6, 1, 7):
        b = (zp + k) % NP
        cb[b] = combined(b)
        sent.append(send(cb.at[b], rb.at[zp], zs.at[k], zr.at[zp], z_dev(2 * b + zb)))
    rb[zp] = combined(zp)

    places = []
    for k in (0, 1, 7, 2, 6, 3, 5, 4):
        q = (zp + k) % NP
        if k:
            arrived(rb.at[q], zr.at[q])
        value = rb[q].astype(F32)
        rf[q] = value
        for o in places:
            put(gp2, q, o, sum_rows(value * rf[o]))
        put(gp2, q, q, sum_rows(value * value))
        places.append(q)

    line = total(line2, slots2, pack(gp2[...]), me_plane, NX * NT, plane_dev, 1)
    line = total(line3, slots3, line, z, NZ, z_dev, 2)
    wv[...] = jnp.broadcast_to(tree_weights(line), wv.shape)
    o_ref[...] = sum(wv[i : i + 1, :] * rf[i] for i in range(NP)).astype(BF16)

    for copy in sent:
        copy.wait_send()


def shards(grad_out, attn_out):
    tok, width = grad_out.shape
    rows, lanes = attn_out.shape
    wide, block = width // GROUP, width // (NX * NZ)
    dma, reg = pltpu.SemaphoreType.DMA, pltpu.VMEM
    return pl.pallas_call(
        kernel,
        out_shape=jax.ShapeDtypeStruct((block, lanes), BF16),
        in_specs=[pl.BlockSpec(memory_space=pl.ANY)] * 2,
        out_specs=pl.BlockSpec(memory_space=pltpu.VMEM),
        scratch_shapes=[
            reg((tok, width), BF16),
            reg((GROUP, tok, wide), BF16),
            reg((GROUP, rows, wide), BF16),
            reg((GROUP, rows, lanes), BF16),
            reg((GROUP, wide, lanes), F32),
            reg((NP, block, lanes), BF16),
            reg((NP, block, lanes), BF16),
            reg((NP, block, lanes), F32),
            reg((8, lanes), F32),
            reg((64, 128), F32),
            reg((64, 128), F32),
            reg((1, 128), F32), reg((GROUP * NT, 128), F32),
            reg((1, 128), F32), reg((NX * NT, 128), F32),
            reg((1, 128), F32), reg((NZ, 128), F32),
            dma((2,)),
            dma((GROUP, 9)), dma((GROUP, 9)),
            dma((11,)), dma((11,)),
            dma((NP,)), dma((NP,)),
            dma((3, 2)),
            pltpu.SemaphoreType.REGULAR((NP // 2 - 1, 5)),
        ],
        compiler_params=pltpu.CompilerParams(
            collective_id=0, has_side_effects=True, vmem_limit_bytes=VMEM
        ),
        name="adasum",
    )(grad_out, attn_out)


def solution(mesh):
    return jax.shard_map(
        shards,
        mesh=mesh,
        in_specs=(P(("dp", "tensor"), None), P("dp", "tensor")),
        out_specs=P("dp", "tensor"),
        check_vma=False,
    )
```

```python
import jax
import jax.numpy as jnp
from jax import lax
from jax.experimental import pallas as pl
from jax.experimental.pallas import tpu as pltpu
from jax.sharding import PartitionSpec as P

MESH = pl.DeviceIdType.MESH
F32 = jnp.float32
BF16 = jnp.bfloat16

NX, NY, NZ = 4, 4, 16
NT = 2 * NY
NP = NZ // 2
GROUP = 2 * NX
EPS = 1e-6
VMEM = 55040 * 1024
ORDER = (0, 1, 3, 4, 5, 7, 2, 6)
AHEAD = 4
ROUNDS = 4
DIRECT = (0, 6)
HEADS = (2, 3, 3, 5, 6)
LAG = 3
HEARS = (0, 1, 3, 5)


def sum_rows(value):
    rows, lanes = value.shape
    part = value.reshape(rows // 8, 8, lanes).sum(axis=0)
    return sum(part[:, i : i + 128] for i in range(0, lanes, 128))


def coef(inner, own_sq):
    return 1.0 - inner / (2.0 * (jnp.maximum(own_sq, 0.0) + EPS))


def pack(lines):
    each = jnp.sum(lines, axis=1, keepdims=True)
    row = lax.broadcasted_iota(jnp.int32, lines.shape, 0)
    lane = lax.broadcasted_iota(jnp.int32, lines.shape, 1)
    return jnp.sum(jnp.where(row == lane, each, 0.0), axis=0, keepdims=True)


def tree_weights(line):
    n = 8
    row = lax.broadcasted_iota(jnp.int32, (n, 128), 0)
    lane = lax.broadcasted_iota(jnp.int32, (n, 128), 1)
    col = lane & (n - 1)
    gram = jnp.where(lane // n == row, jnp.broadcast_to(line, (n, 128)), 0.0)
    for shift in (8, 16, 32, 64):
        gram = gram + pltpu.roll(gram, shift, 1)
    first = lane < n
    weight = None
    step = 1
    while step < n:
        diag, pair = col == row, col == (row ^ step)
        c_row = coef(
            jnp.sum(jnp.where(pair & first, gram, 0.0), axis=1, keepdims=True),
            jnp.sum(jnp.where(diag & first, gram, 0.0), axis=1, keepdims=True),
        )
        weight = c_row if weight is None else weight * c_row
        if 2 * step < n:
            c_col = coef(
                jnp.sum(jnp.where(pair, gram, 0.0), axis=0, keepdims=True),
                jnp.sum(jnp.where(diag, gram, 0.0), axis=0, keepdims=True),
            )
            gram = c_row * gram * c_col
            gram = gram + jnp.where(
                (row & step) != 0, pltpu.roll(gram, step, 0), pltpu.roll(gram, n - step, 0)
            )
            gram = gram + jnp.where(
                (col & step) != 0, pltpu.roll(gram, step, 1), pltpu.roll(gram, 128 - step, 1)
            )
        step *= 2
    return weight


def kernel(
    g_ref, a_ref, o_ref,
    gv, st, gb, ab, lbuf, cb, rb, rf, wv, gp1, gp2,
    line1, slots1, line2, slots2, line3, slots3,
    in_sem, gs, gr, as_, ar, zs, zr, sums, heard,
):
    dp, t = lax.axis_index("dp"), lax.axis_index("tensor")
    z, x = dp // NX, dp % NX
    zp, zb = z // 2, z % 2
    y, c = t // 2, t % 2
    tok = g_ref.shape[0]
    block, lanes = o_ref.shape
    part = block // 2

    def dev(xx, zz, tt):
        return (zz * NX + xx, tt)

    def group_dev(i):
        return dev(i // NT % NX, zp * 2 + i // (NT * NX), i % NT)

    def plane_dev(i):
        return dev(i // NT, z, i % NT)

    def z_dev(i):
        return dev(x, i, t)

    me_group, me_plane = (zb * NX + x) * NT + t, x * NT + t

    def send(src, dst, ssem, rsem, to):
        copy = pltpu.make_async_remote_copy(
            src_ref=src, dst_ref=dst, send_sem=ssem, recv_sem=rsem,
            device_id=to, device_id_type=MESH,
        )
        copy.start()
        return copy

    def arrived(dst, rsem):
        pltpu.make_async_copy(dst, dst, rsem).wait()

    load_g = pltpu.make_async_copy(g_ref, gv, in_sem.at[0])
    load_g.start()
    load_a = pltpu.make_async_copy(a_ref, ab.at[0, c], in_sem.at[1])
    load_a.start()

    barrier = pltpu.get_barrier_semaphore()

    up, down, over = (y + 1) % NY, (y + NY - 1) % NY, (y + 2) % NY
    y_up, y_down, y_over = (dev(x, z, i * 2 + c) for i in (up, down, over))
    core = dev(x, z, y * 2 + 1 - c)
    z_up, z_down = z_dev((z + 2) % NZ), z_dev((z + NZ - 2) % NZ)

    def beside(e):
        return (x + e % NX) % NX, zp * 2 + (zb + e // NX) % 2

    greeted = [dev(*beside(e), 2 * y + i) for e in ORDER[1:] for i in range(2)]
    greeted += [y_up, y_down, y_over, core, z_up, z_down]
    for to in greeted:
        pl.semaphore_signal(barrier, inc=1, device_id=to, device_id_type=MESH)

    load_g.wait()
    for i in range(NX):
        for par in range(2):
            for h in range(2):
                for k in range(0, NP, 4):
                    begins = [64 * (NX * (2 * p + par) + i) + 32 * h for p in range(k, k + 4)]
                    st[par * NX + i, h, :, 32 * k : 32 * k + 128] = jnp.concatenate(
                        [gv[:, b : b + 32] for b in begins], axis=1
                    )
    gb[0, pl.ds(t * tok, tok), :] = st[zb * NX + x, c]
    load_a.wait()
    pl.semaphore_wait(barrier, len(greeted))

    sent, owed = [], []

    chip = 2 * tok

    def rows(yy, begin=0, size=chip):
        return pl.ds(yy * chip + begin, size)

    def give(e):
        xx, zz = beside(e)
        back = e // NX * NX + (NX - e % NX) % NX
        mine = pl.ds(t * tok, tok)
        for i in range(2):
            src = st.at[zz % 2 * NX + xx, i]
            to = dev(xx, zz, 2 * y + i)
            sent.append(send(src, gb.at[back, mine], gs.at[e, i], gr.at[back, c], to))

    def give_core():
        src, dst = st.at[zb * NX + x, 1 - c], gb.at[0, pl.ds(t * tok, tok)]
        sent.append(send(src, dst, gs.at[0, 0], gr.at[0, c], core))

    def spread(e, region, k, to):
        ref = gb.at[e, region]
        sent.append(send(ref, ref, gs.at[e, k], gr.at[e, k], to))

    def landed(e, region, k):
        arrived(gb.at[e, region], gr.at[e, k])

    def start(e):
        landed(e, pl.ds((t + 1 - 2 * c) * tok, tok), 1 - c)
        if e:
            landed(e, pl.ds(t * tok, tok), c)
        spread(e, rows(y), 2, y_up)
        spread(e, rows(y), 3, y_down)
        if e in DIRECT:
            spread(e, rows(y), 4, y_over)

    def near(e):
        landed(e, rows(down), 2)
        if e not in DIRECT:
            spread(e, rows(down, 0, tok), 4, y_up)
        landed(e, rows(up), 3)
        if e not in DIRECT:
            spread(e, rows(up, tok, tok), 5, y_down)

    def far(e):
        if e in DIRECT:
            landed(e, rows(over), 4)
        else:
            landed(e, rows(over, 0, tok), 4)
            landed(e, rows(over, tok, tok), 5)

    arows = ab.shape[2] // 2
    low, high, full = pl.ds(0, arows), pl.ds(arows, arows), pl.ds(0, 2 * arows)
    right, left = dev((x + 1) % NX, z, t), dev((x + 3) % NX, z, t)
    across = dev(x, zp * 2 + 1 - zb, t)

    def pass_on(e, to_e, part, k, to):
        sent.append(send(ab.at[e, c, part], ab.at[to_e, c, part], as_.at[k], ar.at[k], to))

    def have(e, part, k, cc=c):
        arrived(ab.at[e, cc, part], ar.at[k])

    def to_core(e):
        for piece, k in heads_needs.get(e, ()):
            have(e, piece, k)
        pass_on(e, e, full, 11 + e, core)

    def heads_start():
        pass_on(0, 4, full, 2, across)
        pass_on(0, 3, low, 0, right)
        pass_on(0, 1, high, 1, left)

    def heads_second():
        pass_on(0, 3, high, 19, right)
        pass_on(0, 1, low, 20, left)
        to_core(0)

    def heads_near():
        have(3, low, 0)
        pass_on(3, 2, low, 3, right)
        have(1, high, 1)
        pass_on(1, 2, high, 4, left)

    def heads_next():
        have(3, high, 19)
        pass_on(3, 7, high, 5, across)
        have(1, low, 20)
        pass_on(1, 5, low, 6, across)
        to_core(3)
        to_core(1)

    quarters = [pl.ds(i * (arows // 2), arows // 2) for i in range(4)]

    def heads_across():
        have(4, full, 2)
        for i in range(2):
            pass_on(4, 7, quarters[i], 7 + 14 * i, right)
            pass_on(4, 5, quarters[3 - i], 8 + 14 * i, left)
        to_core(4)

    def heads_far(i):
        have(7, quarters[i], 7 + 14 * i)
        pass_on(7, 6, quarters[i], 9 + 14 * i, right)
        have(5, quarters[3 - i], 8 + 14 * i)
        pass_on(5, 6, quarters[3 - i], 10 + 14 * i, left)

    heads_needs = {
        2: ((low, 3), (high, 4)),
        5: ((low, 6),),
        7: ((high, 5),),
        6: ((quarters[0], 9), (quarters[1], 23), (quarters[2], 24), (quarters[3], 10)),
    }

    def index(e):
        return (zb + e // NX) % 2 * NX + (x + e % NX) % NX

    def put(gp, i, j, acc):
        line = jnp.sum(acc, axis=0, keepdims=True)
        gp[pl.ds(i * 8 + j, 1), :] = line
        gp[pl.ds(j * 8 + i, 1), :] = line

    def compute(e, before):
        have(e, full, 11 + e, 1 - c)
        r = index(e)
        both = jnp.concatenate([ab[e, 0], ab[e, 1]], axis=1)
        value = lax.dot_general(
            gb[e], both, (((0,), (0,)), ((), ())), preferred_element_type=F32
        )
        lbuf[r] = value
        for o in before:
            put(gp1, r, index(o), sum_rows(value * lbuf[index(o)]))
        put(gp1, r, r, sum_rows(value * value))

    done = []

    def finish(e):
        far(e)
        compute(e, list(done))
        done.append(e)

    def hear(step):
        if step > 1:
            for side in range(5):
                pl.semaphore_wait(heard.at[step - 2, side], 1)
        if step <= ROUNDS:
            for side, to in enumerate((z_up, z_down, y_up, y_down, core)):
                pl.semaphore_signal(heard.at[step - 1, side], inc=1, device_id=to, device_id_type=MESH)

    for e in ORDER[1:AHEAD]:
        give(e)
    firsts = list(sent)
    hear(1)
    sent.clear()
    give_core()
    start(0)
    for copy in firsts:
        copy.wait_send()
    for e in ORDER[AHEAD:]:
        give(e)
    heads_start()
    for e in ORDER[1:AHEAD]:
        start(e)
    heads_second()
    for i in range(GROUP):
        near(ORDER[i])
        if i + AHEAD < GROUP:
            start(ORDER[i + AHEAD])
        if i == HEADS[0]:
            heads_near()
        if i == HEADS[1]:
            heads_across()
        if i == HEADS[2]:
            heads_next()
        if i == HEADS[3]:
            heads_far(0)
        if i == HEADS[4]:
            heads_far(1)
        if i in HEARS:
            hear(HEARS.index(i) + 2)
        if i >= LAG and i < LAG + 4:
            finish(ORDER[i - LAG])
    rest = [e for e in ORDER if e not in done]
    to_core(rest[0])
    to_core(rest[1])
    to_core(rest[2])
    finish(rest[0])
    to_core(rest[3])
    finish(rest[1])
    finish(rest[2])
    finish(rest[3])

    def total(line, slots, value, me, count, dev_of, k):
        line[...] = value
        keep = pltpu.make_async_copy(line, slots.at[pl.ds(me, 1)], sums.at[k, 1])
        keep.start()

        def out(i, _):
            send(line, slots.at[pl.ds(me, 1)], sums.at[k, 0], sums.at[k, 1], dev_of((me + i) % count))
            return 0

        lax.fori_loop(1, count, out, 0)
        every = slots.at[pl.ds(0, count)]
        pltpu.make_async_copy(every, every, sums.at[k, 1]).wait()
        owed.append((slots.at[pl.ds(0, count - 1)], sums.at[k, 0]))
        return jnp.sum(slots[...], axis=0, keepdims=True)

    line = total(line1, slots1, pack(gp1[...]), me_group, GROUP * NT, group_dev, 0)
    wv[...] = jnp.broadcast_to(tree_weights(line), wv.shape)
    w8 = [wv[i : i + 1, :] for i in range(GROUP)]

    def combined(b):
        region = pl.ds(pl.multiple_of(b * part, part), part)
        return sum(w8[i] * lbuf[i, region, :] for i in range(GROUP)).astype(BF16)

    def offer(k, b, i, to):
        sent.append(send(cb.at[b, i], rb.at[zp, c], zs.at[k, i], zr.at[zp, c], to))

    for k in (4, 3, 5, 2, 6, 1, 7, 0):
        b = (zp + k) % NP
        value = combined(b)
        for i in range(2):
            cb[b, i] = value[:, i * lanes : i * lanes + lanes]
        if k:
            for i in range(2):
                offer(k, b, i, dev(x, 2 * b + zb, 2 * y + i))
        else:
            offer(0, b, 1 - c, core)
    rb[zp, c] = cb[zp, c]

    places = []
    for k in (0, 1, 7, 2, 6, 3, 5, 4):
        q = (zp + k) % NP
        arrived(rb.at[q, 1 - c], zr.at[q, 1 - c])
        if k:
            arrived(rb.at[q, c], zr.at[q, c])
        value = rb[q].astype(F32).reshape(block, lanes)
        rf[q] = value
        for o in places:
            put(gp2, q, o, sum_rows(value * rf[o]))
        put(gp2, q, q, sum_rows(value * value))
        places.append(q)

    line = total(line2, slots2, pack(gp2[...]), me_plane, NX * NT, plane_dev, 1)
    line = total(line3, slots3, line, z, NZ, z_dev, 2)
    wv[...] = jnp.broadcast_to(tree_weights(line), wv.shape)
    o_ref[...] = sum(wv[i : i + 1, :lanes] * rf[i] for i in range(NP)).astype(BF16)

    for copy in sent:
        copy.wait_send()
    for others, sem in owed:
        arrived(others, sem)


def shards(grad_out, attn_out):
    tok, width = grad_out.shape
    rows, lanes = attn_out.shape
    wide, block = width // (2 * GROUP), width // (NX * NZ)
    dma, reg = pltpu.SemaphoreType.DMA, pltpu.VMEM
    return pl.pallas_call(
        kernel,
        out_shape=jax.ShapeDtypeStruct((block, lanes), BF16),
        in_specs=[pl.BlockSpec(memory_space=pl.ANY)] * 2,
        out_specs=pl.BlockSpec(memory_space=pltpu.VMEM),
        scratch_shapes=[
            reg((tok, width), BF16),
            reg((GROUP, 2, tok, wide), BF16),
            reg((GROUP, rows, wide), BF16),
            reg((GROUP, 2, rows, lanes), BF16),
            reg((GROUP, wide, 2 * lanes), F32),
            reg((NP, 2, block // 2, lanes), BF16),
            reg((NP, 2, block // 2, lanes), BF16),
            reg((NP, block, lanes), F32),
            reg((8, 2 * lanes), F32),
            reg((64, 128), F32),
            reg((64, 128), F32),
            reg((1, 128), F32), reg((GROUP * NT, 128), F32),
            reg((1, 128), F32), reg((NX * NT, 128), F32),
            reg((1, 128), F32), reg((NZ, 128), F32),
            dma((2,)),
            dma((GROUP, 6)), dma((GROUP, 6)),
            dma((25,)), dma((25,)),
            dma((NP, 2)), dma((NP, 2)),
            dma((3, 2)),
            pltpu.SemaphoreType.REGULAR((ROUNDS, 5)),
        ],
        compiler_params=pltpu.CompilerParams(
            collective_id=0, has_side_effects=True, vmem_limit_bytes=VMEM
        ),
        name="adasum",
    )(grad_out, attn_out)


def solution(mesh):
    return jax.shard_map(
        shards,
        mesh=mesh,
        in_specs=(P(("dp", "tensor"), None), P("dp", "tensor")),
        out_specs=P("dp", "tensor"),
        check_vma=False,
    )
```

```python
import jax
import jax.numpy as jnp
from jax import lax
from jax.experimental import pallas as pl
from jax.experimental.pallas import tpu as pltpu
from jax.sharding import PartitionSpec as P

MESH = pl.DeviceIdType.MESH
F32 = jnp.float32
BF16 = jnp.bfloat16

NX, NY, NZ = 4, 4, 16
NT = 2 * NY
NP = NZ // 2
GROUP = 2 * NX
EPS = 1e-6
VMEM = 55040 * 1024
ORDER = (0, 1, 3, 4, 5, 7, 2, 6)
AHEAD = 4
ROUNDS = 4
DIRECT = (0, 6)
HEADS = (2, 3, 3, 5, 6)
LAG = 3
HEARS = (0, 1, 3, 5)


def sum_rows(value):
    rows, lanes = value.shape
    part = value.reshape(rows // 8, 8, lanes).sum(axis=0)
    return sum(part[:, i : i + 128] for i in range(0, lanes, 128))


def coef(inner, own_sq):
    return 1.0 - inner / (2.0 * (jnp.maximum(own_sq, 0.0) + EPS))


def pack(lines):
    each = jnp.sum(lines, axis=1, keepdims=True)
    row = lax.broadcasted_iota(jnp.int32, lines.shape, 0)
    lane = lax.broadcasted_iota(jnp.int32, lines.shape, 1)
    return jnp.sum(jnp.where(row == lane, each, 0.0), axis=0, keepdims=True)


def tree_weights(line):
    n = 8
    row = lax.broadcasted_iota(jnp.int32, (n, 128), 0)
    lane = lax.broadcasted_iota(jnp.int32, (n, 128), 1)
    col = lane & (n - 1)
    gram = jnp.where(lane // n == row, jnp.broadcast_to(line, (n, 128)), 0.0)
    for shift in (8, 16, 32, 64):
        gram = gram + pltpu.roll(gram, shift, 1)
    first = lane < n
    weight = None
    step = 1
    while step < n:
        diag, pair = col == row, col == (row ^ step)
        c_row = coef(
            jnp.sum(jnp.where(pair & first, gram, 0.0), axis=1, keepdims=True),
            jnp.sum(jnp.where(diag & first, gram, 0.0), axis=1, keepdims=True),
        )
        weight = c_row if weight is None else weight * c_row
        if 2 * step < n:
            c_col = coef(
                jnp.sum(jnp.where(pair, gram, 0.0), axis=0, keepdims=True),
                jnp.sum(jnp.where(diag, gram, 0.0), axis=0, keepdims=True),
            )
            gram = c_row * gram * c_col
            gram = gram + jnp.where(
                (row & step) != 0, pltpu.roll(gram, step, 0), pltpu.roll(gram, n - step, 0)
            )
            gram = gram + jnp.where(
                (col & step) != 0, pltpu.roll(gram, step, 1), pltpu.roll(gram, 128 - step, 1)
            )
        step *= 2
    return weight


def kernel(
    g_ref, a_ref, o_ref,
    gv, st, gb, ab, lbuf, cb, rb, rf, wv, gp1, gp2,
    line1, slots1, line2, slots2, line3, slots3,
    in_sem, gs, gr, as_, ar, zs, zr, sums, heard,
):
    dp, t = lax.axis_index("dp"), lax.axis_index("tensor")
    z, x = dp // NX, dp % NX
    zp, zb = z // 2, z % 2
    y, c = t // 2, t % 2
    tok = g_ref.shape[0]
    block, lanes = o_ref.shape
    part = block // 2

    def dev(xx, zz, tt):
        return (zz * NX + xx, tt)

    def group_dev(i):
        return dev(i // NT % NX, zp * 2 + i // (NT * NX), i % NT)

    def plane_dev(i):
        return dev(i // NT, z, i % NT)

    def z_dev(i):
        return dev(x, i, t)

    me_group, me_plane = (zb * NX + x) * NT + t, x * NT + t

    def send(src, dst, ssem, rsem, to):
        copy = pltpu.make_async_remote_copy(
            src_ref=src, dst_ref=dst, send_sem=ssem, recv_sem=rsem,
            device_id=to, device_id_type=MESH,
        )
        copy.start()
        return copy

    def arrived(dst, rsem):
        pltpu.make_async_copy(dst, dst, rsem).wait()

    load_g = pltpu.make_async_copy(g_ref, gv, in_sem.at[0])
    load_g.start()
    load_a = pltpu.make_async_copy(a_ref, ab.at[0, c], in_sem.at[1])
    load_a.start()

    barrier = pltpu.get_barrier_semaphore()

    up, down, over = (y + 1) % NY, (y + NY - 1) % NY, (y + 2) % NY
    y_up, y_down, y_over = (dev(x, z, i * 2 + c) for i in (up, down, over))
    core = dev(x, z, y * 2 + 1 - c)
    z_up, z_down = z_dev((z + 2) % NZ), z_dev((z + NZ - 2) % NZ)

    def beside(e):
        return (x + e % NX) % NX, zp * 2 + (zb + e // NX) % 2

    greeted = [dev(*beside(e), 2 * y + i) for e in ORDER[1:] for i in range(2)]
    greeted += [y_up, y_down, y_over, core, z_up, z_down]
    for to in greeted:
        pl.semaphore_signal(barrier, inc=1, device_id=to, device_id_type=MESH)

    load_g.wait()
    for i in range(NX):
        for par in range(2):
            for h in range(2):
                for k in range(0, NP, 4):
                    begins = [64 * (NX * (2 * p + par) + i) + 32 * h for p in range(k, k + 4)]
                    st[par * NX + i, h, :, 32 * k : 32 * k + 128] = jnp.concatenate(
                        [gv[:, b : b + 32] for b in begins], axis=1
                    )
    gb[0, pl.ds(t * tok, tok), :] = st[zb * NX + x, c]
    load_a.wait()
    pl.semaphore_wait(barrier, len(greeted))

    sent, owed = [], []

    chip = 2 * tok

    def rows(yy, begin=0, size=chip):
        return pl.ds(yy * chip + begin, size)

    def give(e):
        xx, zz = beside(e)
        back = e // NX * NX + (NX - e % NX) % NX
        mine = pl.ds(t * tok, tok)
        for i in range(2):
            src = st.at[zz % 2 * NX + xx, i]
            to = dev(xx, zz, 2 * y + i)
            sent.append(send(src, gb.at[back, mine], gs.at[e, i], gr.at[back, c], to))

    def give_core():
        src, dst = st.at[zb * NX + x, 1 - c], gb.at[0, pl.ds(t * tok, tok)]
        sent.append(send(src, dst, gs.at[0, 0], gr.at[0, c], core))

    def spread(e, region, k, to):
        ref = gb.at[e, region]
        sent.append(send(ref, ref, gs.at[e, k], gr.at[e, k], to))

    def landed(e, region, k):
        arrived(gb.at[e, region], gr.at[e, k])

    def start(e):
        landed(e, pl.ds((t + 1 - 2 * c) * tok, tok), 1 - c)
        if e:
            landed(e, pl.ds(t * tok, tok), c)
        spread(e, rows(y), 2, y_up)
        spread(e, rows(y), 3, y_down)
        if e in DIRECT:
            spread(e, rows(y), 4, y_over)

    def near(e):
        landed(e, rows(down), 2)
        if e not in DIRECT:
            spread(e, rows(down, 0, tok), 4, y_up)
        landed(e, rows(up), 3)
        if e not in DIRECT:
            spread(e, rows(up, tok, tok), 5, y_down)

    def far(e):
        if e in DIRECT:
            landed(e, rows(over), 4)
        else:
            landed(e, rows(over, 0, tok), 4)
            landed(e, rows(over, tok, tok), 5)

    arows = ab.shape[2] // 2
    low, high, full = pl.ds(0, arows), pl.ds(arows, arows), pl.ds(0, 2 * arows)
    right, left = dev((x + 1) % NX, z, t), dev((x + 3) % NX, z, t)
    across = dev(x, zp * 2 + 1 - zb, t)

    def pass_on(e, to_e, part, k, to):
        sent.append(send(ab.at[e, c, part], ab.at[to_e, c, part], as_.at[k], ar.at[k], to))

    def have(e, part, k, cc=c):
        arrived(ab.at[e, cc, part], ar.at[k])

    def to_core(e):
        for piece, k in heads_needs.get(e, ()):
            have(e, piece, k)
        pass_on(e, e, full, 11 + e, core)

    def heads_start():
        pass_on(0, 4, full, 2, across)
        pass_on(0, 3, low, 0, right)
        pass_on(0, 1, high, 1, left)

    def heads_second():
        pass_on(0, 3, high, 19, right)
        pass_on(0, 1, low, 20, left)
        to_core(0)

    def heads_near():
        have(3, low, 0)
        pass_on(3, 2, low, 3, right)
        have(1, high, 1)
        pass_on(1, 2, high, 4, left)

    def heads_next():
        have(3, high, 19)
        pass_on(3, 7, high, 5, across)
        have(1, low, 20)
        pass_on(1, 5, low, 6, across)
        to_core(3)
        to_core(1)

    quarters = [pl.ds(i * (arows // 2), arows // 2) for i in range(4)]

    def heads_across():
        have(4, full, 2)
        for i in range(2):
            pass_on(4, 7, quarters[i], 7 + 14 * i, right)
            pass_on(4, 5, quarters[3 - i], 8 + 14 * i, left)
        to_core(4)

    def heads_far(i):
        have(7, quarters[i], 7 + 14 * i)
        pass_on(7, 6, quarters[i], 9 + 14 * i, right)
        have(5, quarters[3 - i], 8 + 14 * i)
        pass_on(5, 6, quarters[3 - i], 10 + 14 * i, left)

    heads_needs = {
        2: ((low, 3), (high, 4)),
        5: ((low, 6),),
        7: ((high, 5),),
        6: ((quarters[0], 9), (quarters[1], 23), (quarters[2], 24), (quarters[3], 10)),
    }

    def index(e):
        return (zb + e // NX) % 2 * NX + (x + e % NX) % NX

    def put(gp, i, j, acc):
        line = jnp.sum(acc, axis=0, keepdims=True)
        gp[pl.ds(i * 8 + j, 1), :] = line
        gp[pl.ds(j * 8 + i, 1), :] = line

    def compute(e, before):
        have(e, full, 11 + e, 1 - c)
        r = index(e)
        both = jnp.concatenate([ab[e, 0], ab[e, 1]], axis=1)
        value = lax.dot_general(
            gb[e], both, (((0,), (0,)), ((), ())), preferred_element_type=F32
        )
        lbuf[r] = value
        for o in before:
            put(gp1, r, index(o), sum_rows(value * lbuf[index(o)]))
        put(gp1, r, r, sum_rows(value * value))

    done = []

    def finish(e):
        far(e)
        compute(e, list(done))
        done.append(e)

    def hear(step):
        if step > 1:
            for side in range(5):
                pl.semaphore_wait(heard.at[step - 2, side], 1)
        if step <= ROUNDS:
            for side, to in enumerate((z_up, z_down, y_up, y_down, core)):
                pl.semaphore_signal(heard.at[step - 1, side], inc=1, device_id=to, device_id_type=MESH)

    for e in ORDER[1:AHEAD]:
        give(e)
    firsts = list(sent)
    hear(1)
    sent.clear()
    give_core()
    start(0)
    for copy in firsts:
        copy.wait_send()
    for e in ORDER[AHEAD:]:
        give(e)
    heads_start()
    heads_second()
    for e in ORDER[1:AHEAD]:
        start(e)
    for i in range(GROUP):
        near(ORDER[i])
        if i + AHEAD < GROUP:
            start(ORDER[i + AHEAD])
        if i == HEADS[0]:
            heads_near()
        if i == HEADS[1]:
            heads_across()
        if i == HEADS[2]:
            heads_next()
        if i == HEADS[3]:
            heads_far(0)
        if i == HEADS[4]:
            heads_far(1)
        if i in HEARS:
            hear(HEARS.index(i) + 2)
        if i >= LAG and i < LAG + 4:
            finish(ORDER[i - LAG])
    rest = [e for e in ORDER if e not in done]
    to_core(rest[0])
    to_core(rest[1])
    to_core(rest[2])
    finish(rest[0])
    to_core(rest[3])
    finish(rest[1])
    finish(rest[2])
    finish(rest[3])

    def settle():
        for copy in sent:
            copy.wait_send()
        for others, sem in owed:
            arrived(others, sem)
        sent.clear()
        owed.clear()

    def total(line, slots, value, me, count, dev_of, k):
        line[...] = value
        keep = pltpu.make_async_copy(line, slots.at[pl.ds(me, 1)], sums.at[k, 1])
        keep.start()

        def out(i, _):
            send(line, slots.at[pl.ds(me, 1)], sums.at[k, 0], sums.at[k, 1], dev_of((me + i) % count))
            return 0

        lax.fori_loop(1, count, out, 0)
        settle()
        every = slots.at[pl.ds(0, count)]
        pltpu.make_async_copy(every, every, sums.at[k, 1]).wait()
        owed.append((slots.at[pl.ds(0, count - 1)], sums.at[k, 0]))
        return jnp.sum(slots[...], axis=0, keepdims=True)

    line = total(line1, slots1, pack(gp1[...]), me_group, GROUP * NT, group_dev, 0)
    wv[...] = jnp.broadcast_to(tree_weights(line), wv.shape)
    w8 = [wv[i : i + 1, :] for i in range(GROUP)]

    def combined(b):
        region = pl.ds(pl.multiple_of(b * part, part), part)
        return sum(w8[i] * lbuf[i, region, :] for i in range(GROUP)).astype(BF16)

    def offer(k, b, i, to):
        sent.append(send(cb.at[b, i], rb.at[zp, c], zs.at[k, i], zr.at[zp, c], to))

    for k in (4, 3, 5, 2, 6, 1, 7, 0):
        b = (zp + k) % NP
        value = combined(b)
        for i in range(2):
            cb[b, i] = value[:, i * lanes : i * lanes + lanes]
        if k:
            for i in range(2):
                offer(k, b, i, dev(x, 2 * b + zb, 2 * y + i))
        else:
            offer(0, b, 1 - c, core)
    rb[zp, c] = cb[zp, c]

    places = []
    for k in (0, 1, 7, 2, 6, 3, 5, 4):
        q = (zp + k) % NP
        arrived(rb.at[q, 1 - c], zr.at[q, 1 - c])
        if k:
            arrived(rb.at[q, c], zr.at[q, c])
        value = rb[q].astype(F32).reshape(block, lanes)
        rf[q] = value
        for o in places:
            put(gp2, q, o, sum_rows(value * rf[o]))
        put(gp2, q, q, sum_rows(value * value))
        places.append(q)

    line = total(line2, slots2, pack(gp2[...]), me_plane, NX * NT, plane_dev, 1)
    line = total(line3, slots3, line, z, NZ, z_dev, 2)
    wv[...] = jnp.broadcast_to(tree_weights(line), wv.shape)
    o_ref[...] = sum(wv[i : i + 1, :lanes] * rf[i] for i in range(NP)).astype(BF16)

    settle()


def shards(grad_out, attn_out):
    tok, width = grad_out.shape
    rows, lanes = attn_out.shape
    wide, block = width // (2 * GROUP), width // (NX * NZ)
    dma, reg = pltpu.SemaphoreType.DMA, pltpu.VMEM
    return pl.pallas_call(
        kernel,
        out_shape=jax.ShapeDtypeStruct((block, lanes), BF16),
        in_specs=[pl.BlockSpec(memory_space=pl.ANY)] * 2,
        out_specs=pl.BlockSpec(memory_space=pltpu.VMEM),
        scratch_shapes=[
            reg((tok, width), BF16),
            reg((GROUP, 2, tok, wide), BF16),
            reg((GROUP, rows, wide), BF16),
            reg((GROUP, 2, rows, lanes), BF16),
            reg((GROUP, wide, 2 * lanes), F32),
            reg((NP, 2, block // 2, lanes), BF16),
            reg((NP, 2, block // 2, lanes), BF16),
            reg((NP, block, lanes), F32),
            reg((8, 2 * lanes), F32),
            reg((64, 128), F32),
            reg((64, 128), F32),
            reg((1, 128), F32), reg((GROUP * NT, 128), F32),
            reg((1, 128), F32), reg((NX * NT, 128), F32),
            reg((1, 128), F32), reg((NZ, 128), F32),
            dma((2,)),
            dma((GROUP, 6)), dma((GROUP, 6)),
            dma((25,)), dma((25,)),
            dma((NP, 2)), dma((NP, 2)),
            dma((3, 2)),
            pltpu.SemaphoreType.REGULAR((ROUNDS, 5)),
        ],
        compiler_params=pltpu.CompilerParams(
            collective_id=0, has_side_effects=True, vmem_limit_bytes=VMEM
        ),
        name="adasum",
    )(grad_out, attn_out)


def solution(mesh):
    return jax.shard_map(
        shards,
        mesh=mesh,
        in_specs=(P(("dp", "tensor"), None), P("dp", "tensor")),
        out_specs=P("dp", "tensor"),
        check_vma=False,
    )
```
